32 devices in a mesh: seq: 8 (over z, x), head: 4 (over y, core).
Axes of the slice: x: 2, y: 2, z: 4, core: 2. Of those that a mesh axis runs over, the one named last changes fastest.
Arguments:
- queries: bfloat16 [12288, 4096], P(('seq', 'head')), may hold values from -32 to 32
- cache_keys: bfloat16 [65536, 1024], P('seq', 'head'), may hold values from -12 to 12
- cache_values: bfloat16 [65536, 1024], P('seq', 'head'), may hold values from -6 to 6
- block_ids: int32 [96, 8], P('seq'), may hold values from 0 to 511, as said below
Outputs:
- attention: bfloat16 [12288, 4096], P(('seq', 'head'))
The draws below stay inside these ranges and needn't reach their ends.
Inputs may be any that keep to these rules, and one draw needn't show every extreme that they name: `block_ids`: entries 0 to 4 of row r name distinct blocks c with c // 64 == r // 12; the other 3 entries name blocks with another value of c // 64, distinct within the row. Among the far entries of the 12 rows with one value of r // 12, at most 6 name blocks of any one other value of c // 64, and exactly 6 do for some value.
All inputs are finite; a program needn't handle non-finite values.
Results may differ from the reference program's by a relative error of at most 0.0043.
Values may be sent and summed in bfloat16 or wider, within the bound.
A program may use at most 128 MiB of HBM per device.

```python
import jax
import jax.numpy as jnp
from jax import lax

QH = 32
KVH = 8
HD = 128
BLK = 128
PICKS = 8
NEAR = 5
QB_DEV = 12
KB_DEV = 64
FAR = 3
CAP = 6
QBLOCKS = 96
KBLOCKS = 512
QTOK = 12288
KTOK = 65536
N_SEQ = 8


def draw_queries(key, part):
    row_count = QB_DEV * BLK * N_SEQ
    column_count = QH * HD
    drawn = jnp.clip(jax.random.normal(jax.random.fold_in(key, 1), (row_count, column_count), jnp.float32), -6.0, 6.0)
    return drawn.astype(jnp.bfloat16)


def draw_cache_keys(key, part):
    row_count = KB_DEV * BLK * N_SEQ
    column_count = KVH * HD
    drawn = jnp.clip(jax.random.normal(jax.random.fold_in(key, 2), (row_count, column_count), jnp.float32), -6.0, 6.0)
    return drawn.astype(jnp.bfloat16)


def draw_block_ids(key, part):

    def one_shard(shard_key, shard_index):
        near_keys = jax.random.split(jax.random.fold_in(shard_key, 1), QB_DEV)
        near_blocks = jax.vmap(lambda near_key: jax.random.permutation(near_key, KB_DEV))(near_keys)[:, :NEAR].astype(jnp.int32)
        others = N_SEQ - 1
        hot_owner = jax.random.randint(jax.random.fold_in(shard_key, 2), (), 0, others, dtype=jnp.int32)
        owner_pool = jnp.repeat(jnp.arange(others, dtype=jnp.int32), CAP)
        shuffle = jax.random.permutation(jax.random.fold_in(shard_key, 3), owner_pool.shape[0]).astype(jnp.int32)
        ordering = jnp.where(owner_pool == hot_owner, shuffle - owner_pool.shape[0], shuffle)
        chosen = owner_pool[jnp.argsort(ordering, stable=True)][:FAR * QB_DEV]
        chosen = chosen[jax.random.permutation(jax.random.fold_in(shard_key, 4), FAR * QB_DEV)]
        owner_of = (shard_index + 1 + chosen) % N_SEQ
        residue = jnp.arange(FAR, dtype=jnp.int32)[None, :]
        within = residue + FAR * jax.random.randint(jax.random.fold_in(shard_key, 5), (QB_DEV, FAR), 0, KB_DEV // FAR, dtype=jnp.int32)
        far_blocks = owner_of.reshape(QB_DEV, FAR) * KB_DEV + within
        return jnp.concatenate([shard_index * KB_DEV + near_blocks, far_blocks], axis=1)
    shard_keys = jax.random.split(key, N_SEQ)
    picked = jax.vmap(one_shard)(shard_keys, jnp.arange(N_SEQ, dtype=jnp.int32))
    return picked.reshape(N_SEQ * QB_DEV, PICKS).astype(jnp.int32)


def steps_of(stream_key, dims, shards, smallest, largest):
    gain, own = 1.0, jax.random.fold_in(stream_key, 6)
    for dim, shards_of in shards:
        heights = jnp.exp(jax.random.uniform(jax.random.fold_in(own, dim), (shards_of,), jnp.float32, smallest / len(shards), largest / len(shards)))
        gain = gain * jnp.repeat(heights, dims[dim] // shards_of).reshape([-1 if axis == dim else 1 for axis in range(len(dims))])
    return gain


def centred(rng, extent, deviation, bound, shards=(), kind=jnp.bfloat16):
    loudness = steps_of(rng, extent, shards, -0.22, 0.18) if shards else 1.0
    entries = jax.random.normal(rng, extent, jnp.float32) * deviation * loudness
    return jnp.minimum(jnp.maximum(entries, -bound), bound).astype(kind)


def setup_inputs(seed: int = 0) -> dict:
    key_list = jax.random.split(jax.random.key(seed), 5)
    queries = draw_queries(jax.random.fold_in(key_list[4], 71), 0)
    cache_keys = draw_cache_keys(jax.random.fold_in(key_list[4], 71), 0)
    cache_values = centred(key_list[2], (KTOK, KVH * HD), 1.0, 6.0, ((0, 8), (1, 4)))
    block_ids = draw_block_ids(jax.random.fold_in(key_list[4], 71), 0)
    return {"queries": queries, "cache_keys": cache_keys, "cache_values": cache_values, "block_ids": block_ids}


def block_partials(query_rows, key_rows, value_rows):
    score_scale = query_rows.shape[-1] ** -0.5
    scores = jnp.einsum("aqgrd,apkgd->apgrqk", query_rows.astype(jnp.float32), key_rows.astype(jnp.float32)) * score_scale
    block_max = jnp.max(scores, axis=-1)
    exponent = jnp.exp(scores - block_max[..., None])
    block_sum = jnp.sum(exponent, axis=-1)
    weight = lax.optimization_barrier(exponent.astype(jnp.bfloat16))
    partial_value = jnp.einsum("apgrqk,apkgd->apqgrd", weight.astype(jnp.float32), value_rows.astype(jnp.float32))
    return partial_value, block_max, block_sum


def merge_picks(partial_value, block_max, block_sum):
    highest = jnp.max(block_max, axis=-4, keepdims=True)
    factor = jnp.exp(block_max - highest)
    denominator = jnp.sum(factor * block_sum, axis=-4)
    numerator = jnp.sum(partial_value * jnp.moveaxis(factor, -1, -3)[..., None], axis=-5)
    return numerator / jnp.moveaxis(denominator, -1, -3)[..., None]


def reference(queries, cache_keys, cache_values, block_ids):
    ratio = QH // KVH
    query_blocks = queries.reshape(QBLOCKS, BLK, KVH, ratio, HD)
    key_blocks = cache_keys.reshape(KBLOCKS, BLK, KVH, HD)
    value_blocks = cache_values.reshape(KBLOCKS, BLK, KVH, HD)

    def attend_block(pieces):
        query_block, picked = pieces
        chosen_keys = jnp.take(key_blocks, picked.astype(jnp.int32), axis=0)
        chosen_values = jnp.take(value_blocks, picked.astype(jnp.int32), axis=0)
        partial_value, block_max, block_sum = block_partials(query_block[None], chosen_keys[None], chosen_values[None])
        return merge_picks(partial_value, block_max, block_sum)[0].astype(jnp.bfloat16)

    combined = lax.map(attend_block, (query_blocks, block_ids))
    return combined.reshape(QTOK, QH * HD)
```

```python
import functools
import math

import jax
import jax.numpy as jnp
from jax import lax
from jax.experimental import pallas as pl
from jax.experimental.pallas import tpu as pltpu
from jax.sharding import PartitionSpec as P

HD = 128
BLK = 128
NEAR = 5
MESH = pl.DeviceIdType.MESH
LOG2E = math.log2(math.e)


def aligned(index, size):
    return pl.ds(pl.multiple_of(index * size, size), size)


def kernel(
    seq_count, head_count, capacity, kv_local, ratio, per_head, far_count,
    ids, asked, queries, keys, values, out,
    k_buf, v_buf, q_buf, got, wanted, send_bufs, recv_bufs, stage,
    id_send, id_recv, q_send, q_recv, f_send, f_recv, o_send, o_recv, o_local, local,
):
    seq = lax.axis_index("seq")
    head = lax.axis_index("head")
    others = seq_count - 1
    rows = queries.shape[0]
    q_width = q_buf.shape[1]
    width = ratio * HD

    def head_peer(step):
        return (head // 2 + step // 2) % 2 * 2 + (head % 2 + step % 2) % 2

    k_load = pltpu.make_async_copy(keys, k_buf, local.at[0])
    v_load = pltpu.make_async_copy(values, v_buf, local.at[1])
    q_own = pltpu.make_async_copy(
        queries.at[:, aligned(head, q_width)], q_buf.at[aligned(head, rows)], local.at[2]
    )
    k_load.start()
    v_load.start()
    q_own.start()

    barrier = pltpu.get_barrier_semaphore()
    for step in range(1, seq_count):
        pl.semaphore_signal(
            barrier, inc=1, device_id={"seq": (seq + step) % seq_count}, device_id_type=MESH
        )
    for step in range(1, head_count):
        pl.semaphore_signal(
            barrier, inc=1, device_id={"head": head_peer(step)}, device_id_type=MESH
        )
    pl.semaphore_wait(barrier, others + head_count - 1)

    def id_copy(step):
        return pltpu.make_async_remote_copy(
            src_ref=asked.at[step],
            dst_ref=got.at[step],
            send_sem=id_send.at[step],
            recv_sem=id_recv.at[step],
            device_id={"seq": (seq + seq_count - 1 - step) % seq_count},
            device_id_type=MESH,
        )

    def q_copy(step):
        peer = head_peer(step)
        return pltpu.make_async_remote_copy(
            src_ref=queries.at[:, aligned(peer, q_width)],
            dst_ref=q_buf.at[aligned(head, rows)],
            send_sem=q_send.at[step - 1],
            recv_sem=q_recv.at[step - 1],
            device_id={"head": peer},
            device_id_type=MESH,
        )

    def far_copy(g, step):
        block = pl.ds(step * capacity, capacity)
        return pltpu.make_async_remote_copy(
            src_ref=send_bufs[g].at[block],
            dst_ref=recv_bufs[g].at[block],
            send_sem=f_send.at[g, step],
            recv_sem=f_recv.at[g, step],
            device_id={"seq": (seq + 1 + step) % seq_count},
            device_id_type=MESH,
        )

    def out_copy(g, step, j):
        peer = head_peer(step)
        return pltpu.make_async_remote_copy(
            src_ref=stage.at[g, peer * per_head + j],
            dst_ref=out.at[aligned(j, BLK), pl.ds(pl.multiple_of(head * q_width + g * width, width), width)],
            send_sem=o_send.at[g, step - 1, j],
            recv_sem=o_recv.at[g, step - 1, j],
            device_id={"head": peer},
            device_id_type=MESH,
        )

    def own_copy(g, j):
        return pltpu.make_async_copy(
            stage.at[g, head * per_head + j],
            out.at[aligned(j, BLK), pl.ds(pl.multiple_of(head * q_width + g * width, width), width)],
            o_local.at[g, j],
        )

    for step in range(others):
        id_copy(step).start()
    for step in range(head_count - 1, 0, -1):
        q_copy(step).start()
    for step in range(others):
        id_copy(step).wait_recv()
    to_scalar = pltpu.make_async_copy(got, wanted, local.at[3])
    to_scalar.start()
    to_scalar.wait()
    k_load.wait()
    v_load.wait()

    def gather(g, step):
        columns = slice(g * HD, (g + 1) * HD)
        for slot in range(capacity):
            block = wanted[step, 0, slot]
            place = step * capacity + slot
            send_bufs[g][place, :, 0:HD] = k_buf[block, :, columns]
            send_bufs[g][place, :, HD:] = v_buf[block, :, columns]

    @pl.loop(0, others)
    def _(step):
        gather(0, step)
        far_copy(0, step).start()

    for g in range(1, kv_local):
        @pl.loop(0, others)
        def _(step):
            gather(g, step)

        @pl.loop(0, others)
        def _(step):
            far_copy(g - 1, step).wait_send()
            far_copy(g, step).start()

    q_own.wait()
    for step in range(1, head_count):
        q_copy(step).wait_recv()

    def attend(g, b):
        columns = slice(g * HD, (g + 1) * HD)
        near = [ids[b, j] for j in range(NEAR)]
        far = [ids[b, NEAR + j] for j in range(far_count)]
        k_all = jnp.concatenate(
            [k_buf[block, :, columns] for block in near]
            + [recv_bufs[g][block, :, 0:HD] for block in far], axis=0
        )
        v_all = jnp.concatenate(
            [v_buf[block, :, columns] for block in near]
            + [recv_bufs[g][block, :, HD:] for block in far], axis=0
        )
        q_rows = q_buf[aligned(b, BLK), g * width:(g + 1) * width]
        pair = 2 if ratio % 2 == 0 else 1
        for first in range(0, ratio, pair):
            q_part = jnp.concatenate(
                [q_rows[:, r * HD:(r + 1) * HD] for r in range(first, first + pair)], axis=0
            )
            scores = lax.dot_general(
                q_part, k_all, (((1,), (1,)), ((), ())), preferred_element_type=jnp.float32
            )
            highest = jnp.max(scores, axis=1, keepdims=True)
            exponent = jnp.exp2((scores - highest) * (HD ** -0.5 * LOG2E))
            total = jnp.sum(exponent, axis=1, keepdims=True)
            mixed = jnp.dot(
                exponent.astype(jnp.bfloat16), v_all, preferred_element_type=jnp.float32
            )
            result = (mixed / total).astype(jnp.bfloat16)
            for r in range(pair):
                stage[g, b, :, (first + r) * HD:(first + r + 1) * HD] = (
                    result[r * BLK:(r + 1) * BLK]
                )

    for g in range(kv_local):
        @pl.loop(0, others)
        def _(step):
            far_copy(g, step).wait_recv()

        @pl.loop(0, (head_count - 1) * per_head)
        def _(index):
            step = head_count - 1 - index // per_head
            j = index % per_head
            attend(g, head_peer(step) * per_head + j)
            out_copy(g, step, j).start()

        @pl.loop(0, per_head)
        def _(j):
            attend(g, head * per_head + j)
            own_copy(g, j).start()

    for step in range(others):
        id_copy(step).wait_send()
        far_copy(kv_local - 1, step).wait_send()
    for step in range(1, head_count):
        q_copy(step).wait_send()
    for g in range(kv_local):
        @pl.loop(0, (head_count - 1) * per_head)
        def _(index):
            step = head_count - 1 - index // per_head
            j = index % per_head
            out_copy(g, step, j).wait()

        @pl.loop(0, per_head)
        def _(j):
            own_copy(g, j).wait()


def shards(queries, cache_keys, cache_values, block_ids):
    seq_count = lax.axis_size("seq")
    head_count = lax.axis_size("head")
    seq = lax.axis_index("seq")
    rows, q_columns = queries.shape
    q_width = q_columns // head_count
    kv_local = cache_keys.shape[1] // HD
    ratio = q_width // (kv_local * HD)
    q_count, picks = block_ids.shape
    per_head = q_count // head_count
    k_count = cache_keys.shape[0] // BLK
    far_count = picks - NEAR
    others = seq_count - 1
    capacity = max(2, (far_count * q_count + seq_count - 2) // others)

    near = block_ids[:, :NEAR] - seq * k_count
    far = block_ids[:, NEAR:].reshape(-1)
    owner = far // k_count
    within = far - owner * k_count
    distance = (seq - owner + seq_count) % seq_count - 1
    order = jnp.arange(far.shape[0], dtype=jnp.int32)
    earlier = (distance[:, None] == distance[None, :]) & (order[None, :] < order[:, None])
    rank = jnp.sum(earlier.astype(jnp.int32), axis=1)
    slot = distance * capacity + rank
    ids = jnp.concatenate([near, slot.reshape(q_count, far_count)], axis=1)
    lane = jnp.arange(128, dtype=jnp.int32)[None, None, None, :]
    shape = (far.shape[0], others, 8, 128)
    hit = (
        (distance[:, None, None, None] == jnp.arange(others, dtype=jnp.int32)[None, :, None, None])
        & (rank[:, None, None, None] == lane)
    )
    asked = jnp.sum(
        jnp.where(jnp.broadcast_to(hit, shape), within[:, None, None, None], 0), axis=0
    )

    slots = others * capacity
    blocks = (k_count, BLK, cache_keys.shape[1])
    bf16 = jnp.bfloat16
    dma = pltpu.SemaphoreType.DMA
    anywhere = pl.BlockSpec(memory_space=pl.ANY)
    return pl.pallas_call(
        functools.partial(
            kernel, seq_count, head_count, capacity, kv_local, ratio, per_head, far_count
        ),
        out_shape=jax.ShapeDtypeStruct((rows, q_columns), bf16),
        in_specs=[
            pl.BlockSpec(memory_space=pltpu.SMEM),
            pl.BlockSpec(memory_space=pltpu.VMEM),
            anywhere, anywhere, anywhere,
        ],
        out_specs=anywhere,
        scratch_shapes=[
            pltpu.VMEM(blocks, bf16),
            pltpu.VMEM(blocks, bf16),
            pltpu.VMEM((rows * head_count, q_width), bf16),
            pltpu.VMEM((others, 8, 128), jnp.int32),
            pltpu.SMEM((others, 8, 128), jnp.int32),
            [pltpu.VMEM((slots, BLK, 2 * HD), bf16) for _ in range(kv_local)],
            [pltpu.VMEM((slots, BLK, 2 * HD), bf16) for _ in range(kv_local)],
            pltpu.VMEM((kv_local, q_count, BLK, ratio * HD), bf16),
            dma((others,)), dma((others,)),
            dma((head_count - 1,)), dma((head_count - 1,)),
            dma((kv_local, others)), dma((kv_local, others)),
            dma((kv_local, head_count - 1, per_head)),
            dma((kv_local, head_count - 1, per_head)),
            dma((kv_local, per_head)),
            dma((4,)),
        ],
        compiler_params=pltpu.CompilerParams(
            collective_id=0, has_side_effects=True, vmem_limit_bytes=56 * 2**20
        ),
    )(ids, asked, queries, cache_keys.reshape(blocks), cache_values.reshape(blocks))


def solution(mesh):
    return jax.shard_map(
        shards,
        mesh=mesh,
        in_specs=(P(("seq", "head"), None), P("seq", "head"), P("seq", "head"), P("seq", None)),
        out_specs=P(("seq", "head"), None),
        check_vma=False,
    )
```

```python
import functools
import math

import jax
import jax.numpy as jnp
from jax import lax
from jax.experimental import pallas as pl
from jax.experimental.pallas import tpu as pltpu
from jax.sharding import PartitionSpec as P

HD = 128
BLK = 128
NEAR = 5
MESH = pl.DeviceIdType.MESH
LOG2E = math.log2(math.e)


def aligned(index, size):
    return pl.ds(pl.multiple_of(index * size, size), size)


def kernel(
    seq_count, head_count, capacity, kv_local, ratio, per_head, far_count,
    ids, asked, queries, keys, values, out,
    k_buf, v_buf, q_buf, got, wanted, send_bufs, recv_bufs, stage,
    id_send, id_recv, q_send, q_recv, f_send, f_recv, o_send, o_recv, o_local, local, turn, near_mixed, near_high, near_total,
):
    seq = lax.axis_index("seq")
    head = lax.axis_index("head")
    others = seq_count - 1
    rows = queries.shape[0]
    q_width = q_buf.shape[1]
    width = ratio * HD

    def head_peer(step):
        return (head // 2 + step // 2) % 2 * 2 + (head % 2 + step % 2) % 2

    k_load = pltpu.make_async_copy(keys, k_buf, local.at[0])
    v_load = pltpu.make_async_copy(values, v_buf, local.at[1])
    q_own = pltpu.make_async_copy(
        queries.at[:, aligned(head, q_width)], q_buf.at[aligned(head, rows)], local.at[2]
    )
    k_load.start()
    v_load.start()
    q_own.start()

    barrier = pltpu.get_barrier_semaphore()
    for step in range(1, seq_count):
        pl.semaphore_signal(
            barrier, inc=1, device_id={"seq": (seq + step) % seq_count}, device_id_type=MESH
        )
    for step in range(1, head_count):
        pl.semaphore_signal(
            barrier, inc=1, device_id={"head": head_peer(step)}, device_id_type=MESH
        )
    pl.semaphore_wait(barrier, others + head_count - 1)

    def id_copy(step):
        return pltpu.make_async_remote_copy(
            src_ref=asked.at[step],
            dst_ref=got.at[step],
            send_sem=id_send.at[step],
            recv_sem=id_recv.at[step],
            device_id={"seq": (seq + seq_count - 1 - step) % seq_count},
            device_id_type=MESH,
        )

    def q_copy(step):
        peer = head_peer(step)
        return pltpu.make_async_remote_copy(
            src_ref=queries.at[:, aligned(peer, q_width)],
            dst_ref=q_buf.at[aligned(head, rows)],
            send_sem=q_send.at[step - 1],
            recv_sem=q_recv.at[step - 1],
            device_id={"head": peer},
            device_id_type=MESH,
        )

    def far_copy(g, step):
        block = pl.ds(step * capacity, capacity)
        return pltpu.make_async_remote_copy(
            src_ref=send_bufs[g].at[block],
            dst_ref=recv_bufs[g].at[block],
            send_sem=f_send.at[g, step],
            recv_sem=f_recv.at[g, step],
            device_id={"seq": (seq + 1 + step) % seq_count},
            device_id_type=MESH,
        )

    def out_copy(g, step, j):
        peer = head_peer(step)
        return pltpu.make_async_remote_copy(
            src_ref=stage.at[g, peer * per_head + j],
            dst_ref=out.at[aligned(j, BLK), pl.ds(pl.multiple_of(head * q_width + g * width, width), width)],
            send_sem=o_send.at[g, step - 1, j],
            recv_sem=o_recv.at[g, step - 1, j],
            device_id={"head": peer},
            device_id_type=MESH,
        )

    def own_copy(g, j):
        return pltpu.make_async_copy(
            stage.at[g, head * per_head + j],
            out.at[aligned(j, BLK), pl.ds(pl.multiple_of(head * q_width + g * width, width), width)],
            o_local.at[g, j],
        )

    for step in range(others):
        id_copy(step).start()
    for step in range(head_count - 1, 0, -1):
        q_copy(step).start()
    for step in range(others):
        id_copy(step).wait_recv()
    to_scalar = pltpu.make_async_copy(got, wanted, local.at[3])
    to_scalar.start()
    to_scalar.wait()
    k_load.wait()
    v_load.wait()

    def gather(g, step):
        columns = slice(g * HD, (g + 1) * HD)
        for slot in range(capacity):
            block = wanted[step, 0, slot]
            place = step * capacity + slot
            send_bufs[g][place, :, 0:HD] = k_buf[block, :, columns]
            send_bufs[g][place, :, HD:] = v_buf[block, :, columns]

    core = head % 2

    @pl.when(core == 0)
    def _():
        @pl.loop(0, others)
        def _(step):
            gather(0, step)
            far_copy(0, step).start()

    @pl.when(core == 1)
    def _():
        @pl.loop(0, others)
        def _(step):
            gather(0, step)

    for g in range(1, kv_local):
        @pl.loop(0, others)
        def _(step):
            gather(g, step)

    def advance(g):
        @pl.loop(0, others)
        def _(step):
            far_copy(g, step).wait_send()
            if g + 1 < kv_local:
                far_copy(g + 1, step).start()

    @pl.when(core == 0)
    def _():
        @pl.loop(0, others)
        def _(step):
            far_copy(0, step).wait_send()
            pl.semaphore_signal(
                turn.at[step], inc=1, device_id={"head": head_peer(1)}, device_id_type=MESH
            )
            if kv_local > 1:
                far_copy(1, step).start()

    @pl.when(core == 1)
    def _():
        @pl.loop(0, others)
        def _(step):
            pl.semaphore_wait(turn.at[step], 1)
            far_copy(0, step).start()

    q_own.wait()
    for step in range(1, head_count):
        q_copy(step).wait_recv()

    pair = 2 if ratio % 2 == 0 else 1
    scale = HD ** -0.5 * LOG2E

    def query_parts(g, b):
        q_rows = q_buf[aligned(b, BLK), g * width:(g + 1) * width]
        for first in range(0, ratio, pair):
            yield first, jnp.concatenate(
                [q_rows[:, r * HD:(r + 1) * HD] for r in range(first, first + pair)], axis=0
            )

    def scores_of(q_part, k_all):
        return lax.dot_general(
            q_part, k_all, (((1,), (1,)), ((), ())), preferred_element_type=jnp.float32
        )

    def near_part(g, b):
        columns = slice(g * HD, (g + 1) * HD)
        near = [ids[b, j] for j in range(NEAR)]
        k_all = jnp.concatenate([k_buf[block, :, columns] for block in near], axis=0)
        v_all = jnp.concatenate([v_buf[block, :, columns] for block in near], axis=0)
        for first, q_part in query_parts(g, b):
            scores = scores_of(q_part, k_all)
            highest = jnp.max(scores, axis=1, keepdims=True)
            exponent = jnp.exp2((scores - highest) * scale)
            total = jnp.sum(exponent, axis=1, keepdims=True)
            mixed = jnp.dot(
                exponent.astype(jnp.bfloat16), v_all, preferred_element_type=jnp.float32
            )
            rows_of = pl.ds(first * BLK, pair * BLK)
            near_mixed[g, b, rows_of, :] = mixed
            near_high[g, b, rows_of, :] = jnp.broadcast_to(highest, mixed.shape)
            near_total[g, b, rows_of, :] = jnp.broadcast_to(total, mixed.shape)

    def far_part(g, b):
        far = [ids[b, NEAR + j] for j in range(far_count)]
        k_all = jnp.concatenate([recv_bufs[g][block, :, 0:HD] for block in far], axis=0)
        v_all = jnp.concatenate([recv_bufs[g][block, :, HD:] for block in far], axis=0)
        for first, q_part in query_parts(g, b):
            rows_of = pl.ds(first * BLK, pair * BLK)
            scores = scores_of(q_part, k_all)
            before = near_high[g, b, rows_of, :]
            highest = jnp.maximum(before, jnp.max(scores, axis=1, keepdims=True))
            factor = jnp.exp2((before - highest) * scale)
            exponent = jnp.concatenate(
                [
                    jnp.exp2((scores[:, j * BLK:(j + 1) * BLK] - highest) * scale)
                    for j in range(far_count)
                ],
                axis=1,
            )
            total = near_total[g, b, rows_of, :] * factor + jnp.sum(exponent, axis=1, keepdims=True)
            mixed = near_mixed[g, b, rows_of, :] * factor + jnp.dot(
                exponent.astype(jnp.bfloat16), v_all, preferred_element_type=jnp.float32
            )
            result = (mixed / total).astype(jnp.bfloat16)
            for r in range(pair):
                stage[g, b, :, (first + r) * HD:(first + r + 1) * HD] = (
                    result[r * BLK:(r + 1) * BLK]
                )

    for g in range(kv_local):
        @pl.loop(0, head_count * per_head)
        def _(b):
            near_part(g, b)

    for g in range(kv_local):
        if g + 1 < kv_local:
            if g == 0:
                @pl.when(core == 1)
                def _():
                    advance(0)
            else:
                advance(g)

        @pl.loop(0, others)
        def _(step):
            far_copy(g, step).wait_recv()

        @pl.loop(0, (head_count - 1) * per_head)
        def _(index):
            step = head_count - 1 - index // per_head
            j = index % per_head
            far_part(g, head_peer(step) * per_head + j)
            out_copy(g, step, j).start()

        @pl.loop(0, per_head)
        def _(j):
            far_part(g, head * per_head + j)
            own_copy(g, j).start()

    for step in range(others):
        id_copy(step).wait_send()
        far_copy(kv_local - 1, step).wait_send()
    for step in range(1, head_count):
        q_copy(step).wait_send()
    for g in range(kv_local):
        @pl.loop(0, (head_count - 1) * per_head)
        def _(index):
            step = head_count - 1 - index // per_head
            j = index % per_head
            out_copy(g, step, j).wait()

        @pl.loop(0, per_head)
        def _(j):
            own_copy(g, j).wait()


def shards(queries, cache_keys, cache_values, block_ids):
    seq_count = lax.axis_size("seq")
    head_count = lax.axis_size("head")
    seq = lax.axis_index("seq")
    rows, q_columns = queries.shape
    q_width = q_columns // head_count
    kv_local = cache_keys.shape[1] // HD
    ratio = q_width // (kv_local * HD)
    q_count, picks = block_ids.shape
    per_head = q_count // head_count
    k_count = cache_keys.shape[0] // BLK
    far_count = picks - NEAR
    others = seq_count - 1
    capacity = max(2, (far_count * q_count + seq_count - 2) // others)

    near = block_ids[:, :NEAR] - seq * k_count
    far = block_ids[:, NEAR:].reshape(-1)
    owner = far // k_count
    within = far - owner * k_count
    distance = (seq - owner + seq_count) % seq_count - 1
    order = jnp.arange(far.shape[0], dtype=jnp.int32)
    earlier = (distance[:, None] == distance[None, :]) & (order[None, :] < order[:, None])
    rank = jnp.sum(earlier.astype(jnp.int32), axis=1)
    slot = distance * capacity + rank
    ids = jnp.concatenate([near, slot.reshape(q_count, far_count)], axis=1)
    lane = jnp.arange(128, dtype=jnp.int32)[None, None, None, :]
    shape = (far.shape[0], others, 8, 128)
    hit = (
        (distance[:, None, None, None] == jnp.arange(others, dtype=jnp.int32)[None, :, None, None])
        & (rank[:, None, None, None] == lane)
    )
    asked = jnp.sum(
        jnp.where(jnp.broadcast_to(hit, shape), within[:, None, None, None], 0), axis=0
    )

    slots = others * capacity
    blocks = (k_count, BLK, cache_keys.shape[1])
    bf16 = jnp.bfloat16
    dma = pltpu.SemaphoreType.DMA
    anywhere = pl.BlockSpec(memory_space=pl.ANY)
    return pl.pallas_call(
        functools.partial(
            kernel, seq_count, head_count, capacity, kv_local, ratio, per_head, far_count
        ),
        out_shape=jax.ShapeDtypeStruct((rows, q_columns), bf16),
        in_specs=[
            pl.BlockSpec(memory_space=pltpu.SMEM),
            pl.BlockSpec(memory_space=pltpu.VMEM),
            anywhere, anywhere, anywhere,
        ],
        out_specs=anywhere,
        scratch_shapes=[
            pltpu.VMEM(blocks, bf16),
            pltpu.VMEM(blocks, bf16),
            pltpu.VMEM((rows * head_count, q_width), bf16),
            pltpu.VMEM((others, 8, 128), jnp.int32),
            pltpu.SMEM((others, 8, 128), jnp.int32),
            [pltpu.VMEM((slots, BLK, 2 * HD), bf16) for _ in range(kv_local)],
            [pltpu.VMEM((slots, BLK, 2 * HD), bf16) for _ in range(kv_local)],
            pltpu.VMEM((kv_local, q_count, BLK, ratio * HD), bf16),
            dma((others,)), dma((others,)),
            dma((head_count - 1,)), dma((head_count - 1,)),
            dma((kv_local, others)), dma((kv_local, others)),
            dma((kv_local, head_count - 1, per_head)),
            dma((kv_local, head_count - 1, per_head)),
            dma((kv_local, per_head)),
            dma((4,)),
            pltpu.SemaphoreType.REGULAR((others,)),
            pltpu.VMEM((kv_local, q_count, ratio * BLK, HD), jnp.float32),
            pltpu.VMEM((kv_local, q_count, ratio * BLK, HD), jnp.float32),
            pltpu.VMEM((kv_local, q_count, ratio * BLK, HD), jnp.float32),
        ],
        compiler_params=pltpu.CompilerParams(
            collective_id=0, has_side_effects=True, vmem_limit_bytes=56 * 2**20
        ),
    )(ids, asked, queries, cache_keys.reshape(blocks), cache_values.reshape(blocks))


def solution(mesh):
    return jax.shard_map(
        shards,
        mesh=mesh,
        in_specs=(P(("seq", "head"), None), P("seq", "head"), P("seq", "head"), P("seq", None)),
        out_specs=P(("seq", "head"), None),
        check_vma=False,
    )
```

```python
import functools
import math

import jax
import jax.numpy as jnp
from jax import lax
from jax.experimental import pallas as pl
from jax.experimental.pallas import tpu as pltpu
from jax.sharding import PartitionSpec as P

HD = 128
BLK = 128
NEAR = 5
PIECES = 8
MESH = pl.DeviceIdType.MESH
LOG2E = math.log2(math.e)


def aligned(index, size):
    return pl.ds(pl.multiple_of(index * size, size), size)


def kernel(
    seq_count, head_count, capacity, kv_local, ratio, per_head, far_count,
    ids, slots_of, asked, queries, keys, values, out,
    k_buf, v_buf, q_buf, got, wanted, send_bufs, recv_bufs, stage,
    id_send, id_recv, q_send, q_recv, f_send, f_recv, o_send, o_recv, o_local, local, near_mixed, near_high, near_total,
):
    seq = lax.axis_index("seq")
    head = lax.axis_index("head")
    others = seq_count - 1
    rows = queries.shape[0]
    q_width = q_buf.shape[1]
    width = ratio * HD

    def seq_peer(step):
        peer = 0
        weight = 1
        while weight < seq_count:
            peer += (seq // weight + (step + 1) // weight) % 2 * weight
            weight *= 2
        return peer

    def head_peer(step):
        return (head // 2 + step // 2) % 2 * 2 + (head % 2 + step % 2) % 2

    k_load = pltpu.make_async_copy(keys, k_buf, local.at[0])
    v_load = pltpu.make_async_copy(values, v_buf, local.at[1])
    q_own = pltpu.make_async_copy(
        queries.at[:, aligned(head, q_width)], q_buf.at[aligned(head, rows)], local.at[2]
    )
    k_load.start()
    v_load.start()
    q_own.start()

    barrier = pltpu.get_barrier_semaphore()
    for step in range(others):
        pl.semaphore_signal(
            barrier, inc=1, device_id={"seq": seq_peer(step)}, device_id_type=MESH
        )
    for step in range(1, head_count):
        pl.semaphore_signal(
            barrier, inc=1, device_id={"head": head_peer(step)}, device_id_type=MESH
        )
    pl.semaphore_wait(barrier, others + head_count - 1)

    def id_copy(step):
        return pltpu.make_async_remote_copy(
            src_ref=asked.at[step],
            dst_ref=got.at[step],
            send_sem=id_send.at[step],
            recv_sem=id_recv.at[step],
            device_id={"seq": seq_peer(step)},
            device_id_type=MESH,
        )

    def q_copy(step):
        peer = head_peer(step)
        return pltpu.make_async_remote_copy(
            src_ref=queries.at[:, aligned(peer, q_width)],
            dst_ref=q_buf.at[aligned(head, rows)],
            send_sem=q_send.at[step - 1],
            recv_sem=q_recv.at[step - 1],
            device_id={"head": peer},
            device_id_type=MESH,
        )

    def far_copy(g, step):
        block = pl.ds(step * capacity, capacity)
        return pltpu.make_async_remote_copy(
            src_ref=send_bufs[g].at[block],
            dst_ref=recv_bufs[g].at[block],
            send_sem=f_send.at[g, step],
            recv_sem=f_recv.at[g, step],
            device_id={"seq": seq_peer(step)},
            device_id_type=MESH,
        )

    def out_copy(g, step, j):
        peer = head_peer(step)
        return pltpu.make_async_remote_copy(
            src_ref=stage.at[g, peer * per_head + j],
            dst_ref=out.at[aligned(j, BLK), pl.ds(pl.multiple_of(head * q_width + g * width, width), width)],
            send_sem=o_send.at[g, step - 1, j],
            recv_sem=o_recv.at[g, step - 1, j],
            device_id={"head": peer},
            device_id_type=MESH,
        )

    def own_copy(g, j):
        return pltpu.make_async_copy(
            stage.at[g, head * per_head + j],
            out.at[aligned(j, BLK), pl.ds(pl.multiple_of(head * q_width + g * width, width), width)],
            o_local.at[g, j],
        )

    for step in range(others):
        id_copy(step).start()
    for step in range(head_count - 1, 0, -1):
        q_copy(step).start()
    for step in range(others):
        id_copy(step).wait_recv()
    to_scalar = pltpu.make_async_copy(got, wanted, local.at[3])
    to_scalar.start()
    to_scalar.wait()
    k_load.wait()
    v_load.wait()

    def gather(g, step):
        columns = slice(g * HD, (g + 1) * HD)
        for slot in range(capacity):
            block = wanted[step, 0, slot]
            place = step * capacity + slot
            send_bufs[g][place, :, 0:HD] = k_buf[block, :, columns]
            send_bufs[g][place, :, HD:] = v_buf[block, :, columns]

    core = head % 2

    def peer_at(index):
        turned = (index + core) % others
        odd = turned % 2
        return (1 - odd) * (seq_count // 2 + turned // 2) + odd * ((turned + 1) // 2) - 1

    @pl.loop(0, others)
    def _(index):
        step = peer_at(index)
        gather(0, step)
        far_copy(0, step).start()

    for g in range(1, kv_local):
        @pl.loop(0, others)
        def _(step):
            gather(g, step)

    def advance(g):
        @pl.loop(0, others)
        def _(index):
            step = peer_at(index)
            far_copy(g, step).wait_send()
            far_copy(g + 1, step).start()

    if kv_local > 1:
        advance(0)

    q_own.wait()
    for step in range(1, head_count):
        q_copy(step).wait_recv()

    pair = 2 if ratio % 2 == 0 else 1
    scale = HD ** -0.5 * LOG2E

    def query_parts(g, b):
        q_rows = q_buf[aligned(b, BLK), g * width:(g + 1) * width]
        for first in range(0, ratio, pair):
            yield first, jnp.concatenate(
                [q_rows[:, r * HD:(r + 1) * HD] for r in range(first, first + pair)], axis=0
            )

    def scores_of(q_part, k_all):
        return lax.dot_general(
            q_part, k_all, (((1,), (1,)), ((), ())), preferred_element_type=jnp.float32
        )

    def near_part(g, b):
        columns = slice(g * HD, (g + 1) * HD)
        near = [lax.rem(ids[j, b], k_buf.shape[0]) for j in range(NEAR)]
        k_all = jnp.concatenate([k_buf[block, :, columns] for block in near], axis=0)
        v_all = jnp.concatenate([v_buf[block, :, columns] for block in near], axis=0)
        for first, q_part in query_parts(g, b):
            scores = scores_of(q_part, k_all)
            highest = jnp.max(scores, axis=1, keepdims=True)
            exponent = jnp.exp2((scores - highest) * scale)
            total = jnp.sum(exponent, axis=1, keepdims=True)
            mixed = jnp.dot(
                exponent.astype(jnp.bfloat16), v_all, preferred_element_type=jnp.float32
            )
            rows_of = pl.ds(first * BLK, pair * BLK)
            near_mixed[g, b, rows_of, :] = mixed
            near_high[g, b, rows_of, :] = jnp.broadcast_to(highest, mixed.shape)
            near_total[g, b, rows_of, :] = jnp.broadcast_to(total, mixed.shape)

    def far_part(g, b):
        far = [slots_of[j, b] for j in range(far_count)]
        k_all = jnp.concatenate([recv_bufs[g][block, :, 0:HD] for block in far], axis=0)
        v_all = jnp.concatenate([recv_bufs[g][block, :, HD:] for block in far], axis=0)
        for first, q_part in query_parts(g, b):
            rows_of = pl.ds(first * BLK, pair * BLK)
            scores = scores_of(q_part, k_all)
            before = near_high[g, b, rows_of, :]
            highest = jnp.maximum(before, jnp.max(scores, axis=1, keepdims=True))
            factor = jnp.exp2((before - highest) * scale)
            exponent = jnp.concatenate(
                [
                    jnp.exp2((scores[:, j * BLK:(j + 1) * BLK] - highest) * scale)
                    for j in range(far_count)
                ],
                axis=1,
            )
            total = near_total[g, b, rows_of, :] * factor + jnp.sum(exponent, axis=1, keepdims=True)
            mixed = near_mixed[g, b, rows_of, :] * factor + jnp.dot(
                exponent.astype(jnp.bfloat16), v_all, preferred_element_type=jnp.float32
            )
            result = (mixed / total).astype(jnp.bfloat16)
            for r in range(pair):
                stage[g, b, :, (first + r) * HD:(first + r + 1) * HD] = (
                    result[r * BLK:(r + 1) * BLK]
                )

    for g in range(kv_local):
        @pl.loop(0, head_count * per_head)
        def _(b):
            near_part(g, b)

    for g in range(kv_local):
        if 0 < g < kv_local - 1:
            advance(g)

        @pl.loop(0, others)
        def _(step):
            far_copy(g, step).wait_recv()

        @pl.loop(0, (head_count - 1) * per_head)
        def _(index):
            step = head_count - 1 - index // per_head
            j = index % per_head
            far_part(g, head_peer(step) * per_head + j)
            out_copy(g, step, j).start()

        @pl.loop(0, per_head)
        def _(j):
            far_part(g, head * per_head + j)
            own_copy(g, j).start()

    for step in range(others):
        id_copy(step).wait_send()
        far_copy(kv_local - 1, step).wait_send()
    for step in range(1, head_count):
        q_copy(step).wait_send()
    for g in range(kv_local):
        @pl.loop(0, (head_count - 1) * per_head)
        def _(index):
            step = head_count - 1 - index // per_head
            j = index % per_head
            out_copy(g, step, j).wait()

        @pl.loop(0, per_head)
        def _(j):
            own_copy(g, j).wait()


def hand_over(landed, out, done):
    size = out.shape[0] // PIECES
    copies = [
        pltpu.make_async_copy(
            landed.at[pl.ds(piece * size, size)], out.at[pl.ds(piece * size, size)], done.at[piece]
        )
        for piece in range(PIECES)
    ]
    for copy in copies:
        copy.start()
    for copy in copies:
        copy.wait()


def shards(queries, cache_keys, cache_values, block_ids):
    seq_count = lax.axis_size("seq")
    head_count = lax.axis_size("head")
    seq = lax.axis_index("seq")
    rows, q_columns = queries.shape
    q_width = q_columns // head_count
    kv_local = cache_keys.shape[1] // HD
    ratio = q_width // (kv_local * HD)
    q_count, picks = block_ids.shape
    per_head = q_count // head_count
    k_count = cache_keys.shape[0] // BLK
    far_count = picks - NEAR
    others = seq_count - 1
    capacity = max(2, (far_count * q_count + seq_count - 2) // others)

    ids = block_ids.T
    far = ids[NEAR:].reshape(-1)
    owner = far // k_count
    within = far - owner * k_count
    distance = (seq ^ owner) - 1
    order = jnp.arange(far.shape[0], dtype=jnp.int32)
    earlier = (distance[:, None] == distance[None, :]) & (order[None, :] < order[:, None])
    rank = jnp.sum(earlier.astype(jnp.int32), axis=1)
    slot = distance * capacity + rank
    slots_of = slot.reshape(far_count, q_count)
    lane = jnp.arange(128, dtype=jnp.int32)[None, None, None, :]
    shape = (far.shape[0], others, 8, 128)
    hit = (
        (distance[:, None, None, None] == jnp.arange(others, dtype=jnp.int32)[None, :, None, None])
        & (rank[:, None, None, None] == lane)
    )
    asked = jnp.sum(
        jnp.where(jnp.broadcast_to(hit, shape), within[:, None, None, None], 0), axis=0
    )

    slots = others * capacity
    blocks = (k_count, BLK, cache_keys.shape[1])
    bf16 = jnp.bfloat16
    dma = pltpu.SemaphoreType.DMA
    anywhere = pl.BlockSpec(memory_space=pl.ANY)
    landed = pl.pallas_call(
        functools.partial(
            kernel, seq_count, head_count, capacity, kv_local, ratio, per_head, far_count
        ),
        out_shape=jax.ShapeDtypeStruct((rows, q_columns), bf16),
        in_specs=[
            pl.BlockSpec(memory_space=pltpu.SMEM),
            pl.BlockSpec(memory_space=pltpu.SMEM),
            pl.BlockSpec(memory_space=pltpu.VMEM),
            anywhere, anywhere, anywhere,
        ],
        out_specs=anywhere,
        scratch_shapes=[
            pltpu.VMEM(blocks, bf16),
            pltpu.VMEM(blocks, bf16),
            pltpu.VMEM((rows * head_count, q_width), bf16),
            pltpu.VMEM((others, 8, 128), jnp.int32),
            pltpu.SMEM((others, 8, 128), jnp.int32),
            [pltpu.VMEM((slots, BLK, 2 * HD), bf16) for _ in range(kv_local)],
            [pltpu.VMEM((slots, BLK, 2 * HD), bf16) for _ in range(kv_local)],
            pltpu.VMEM((kv_local, q_count, BLK, ratio * HD), bf16),
            dma((others,)), dma((others,)),
            dma((head_count - 1,)), dma((head_count - 1,)),
            dma((kv_local, others)), dma((kv_local, others)),
            dma((kv_local, head_count - 1, per_head)),
            dma((kv_local, head_count - 1, per_head)),
            dma((kv_local, per_head)),
            dma((4,)),
            pltpu.VMEM((kv_local, q_count, ratio * BLK, HD), jnp.float32),
            pltpu.VMEM((kv_local, q_count, ratio * BLK, HD), jnp.float32),
            pltpu.VMEM((kv_local, q_count, ratio * BLK, HD), jnp.float32),
        ],
        compiler_params=pltpu.CompilerParams(
            collective_id=0, has_side_effects=True, vmem_limit_bytes=56 * 2**20
        ),
    )(ids, slots_of, asked, queries, cache_keys.reshape(blocks), cache_values.reshape(blocks))
    return pl.pallas_call(
        hand_over,
        out_shape=jax.ShapeDtypeStruct((rows, q_columns), bf16),
        in_specs=[anywhere],
        out_specs=anywhere,
        scratch_shapes=[dma((PIECES,))],
        compiler_params=pltpu.CompilerParams(vmem_limit_bytes=62 * 2**20),
    )(landed)


def solution(mesh):
    return jax.shard_map(
        shards,
        mesh=mesh,
        in_specs=(P(("seq", "head"), None), P("seq", "head"), P("seq", "head"), P("seq", None)),
        out_specs=P(("seq", "head"), None),
        check_vma=False,
    )
```

```python
import functools
import math

import jax
import jax.numpy as jnp
from jax import lax
from jax.experimental import pallas as pl
from jax.experimental.pallas import tpu as pltpu
from jax.sharding import PartitionSpec as P

HD = 128
BLK = 128
NEAR = 5
TILE = 64
MESH = pl.DeviceIdType.MESH
LOG2E = math.log2(math.e)


def aligned(index, size):
    return pl.ds(pl.multiple_of(index * size, size), size)


def kernel(
    seq_count, head_count, capacity, kv_local, ratio, per_head, far_count,
    ids, slots_of, asked, queries, keys, values, *rest
):
    landed, rest = rest[:kv_local + 1], rest[kv_local + 1:]
    (
        k_buf, v_buf, q_buf, got, wanted, send_bufs, recv_bufs, stages,
        id_send, id_recv, q_send, q_recv, f_send, f_recv, o_send, o_recv, o_local, local,
        near_mixed, near_high, near_total, far_weight,
    ) = rest
    seq = lax.axis_index("seq")
    head = lax.axis_index("head")
    others = seq_count - 1
    rows = queries.shape[0]
    q_width = q_buf.shape[1]
    width = ratio * HD
    last = kv_local - 1
    half = HD // 2

    def seq_peer(step):
        peer = 0
        weight = 1
        while weight < seq_count:
            peer += (seq // weight + (step + 1) // weight) % 2 * weight
            weight *= 2
        return peer

    def head_peer(step):
        return (head // 2 + step // 2) % 2 * 2 + (head % 2 + step % 2) % 2

    k_load = pltpu.make_async_copy(keys, k_buf, local.at[0])
    v_load = pltpu.make_async_copy(values, v_buf, local.at[1])
    q_own = pltpu.make_async_copy(
        queries.at[:, aligned(head, q_width)], q_buf.at[aligned(head, rows)], local.at[2]
    )
    k_load.start()
    v_load.start()
    q_own.start()

    barrier = pltpu.get_barrier_semaphore()
    for step in range(others):
        pl.semaphore_signal(
            barrier, inc=1, device_id={"seq": seq_peer(step)}, device_id_type=MESH
        )
    for step in range(1, head_count):
        pl.semaphore_signal(
            barrier, inc=1, device_id={"head": head_peer(step)}, device_id_type=MESH
        )
    pl.semaphore_wait(barrier, others + head_count - 1)

    def id_copy(step):
        return pltpu.make_async_remote_copy(
            src_ref=asked.at[step],
            dst_ref=got.at[step],
            send_sem=id_send.at[step],
            recv_sem=id_recv.at[step],
            device_id={"seq": seq_peer(step)},
            device_id_type=MESH,
        )

    def q_copy(step):
        peer = head_peer(step)
        return pltpu.make_async_remote_copy(
            src_ref=queries.at[:, aligned(peer, q_width)],
            dst_ref=q_buf.at[aligned(head, rows)],
            send_sem=q_send.at[step - 1],
            recv_sem=q_recv.at[step - 1],
            device_id={"head": peer},
            device_id_type=MESH,
        )

    def far_copy(g, step):
        block = pl.ds(step * capacity, capacity)
        return pltpu.make_async_remote_copy(
            src_ref=send_bufs[g].at[block],
            dst_ref=recv_bufs[g].at[block],
            send_sem=f_send.at[g, step],
            recv_sem=f_recv.at[g, step],
            device_id={"seq": seq_peer(step)},
            device_id_type=MESH,
        )

    def place(part, j):
        span = stages[part].shape[2]
        return landed[part].at[aligned(j, BLK), aligned(head, span)]

    def out_copy(part, step, j):
        peer = head_peer(step)
        return pltpu.make_async_remote_copy(
            src_ref=stages[part].at[peer * per_head + j],
            dst_ref=place(part, j),
            send_sem=o_send.at[part, step - 1, j],
            recv_sem=o_recv.at[part, step - 1, j],
            device_id={"head": peer},
            device_id_type=MESH,
        )

    def own_copy(part, j):
        return pltpu.make_async_copy(
            stages[part].at[head * per_head + j], place(part, j), o_local.at[part, j]
        )

    for step in range(others):
        id_copy(step).start()
    for step in range(head_count - 1, 0, -1):
        q_copy(step).start()
    for step in range(others):
        id_copy(step).wait_recv()
    to_scalar = pltpu.make_async_copy(got, wanted, local.at[3])
    to_scalar.start()
    to_scalar.wait()
    k_load.wait()
    v_load.wait()

    def gather(g, step):
        columns = slice(g * HD, (g + 1) * HD)
        for slot in range(capacity):
            block = wanted[step, 0, slot]
            spot = step * capacity + slot
            if g < last:
                send_bufs[g][spot, :, 0:HD] = k_buf[block, :, columns]
                send_bufs[g][spot, :, HD:] = v_buf[block, :, columns]
            else:
                send_bufs[g][spot] = k_buf[block, :, columns]
                value = v_buf[block, :, columns]
                for part in range(2):
                    side = value[:, part * half:(part + 1) * half]
                    send_bufs[g + 1 + part][spot] = jnp.concatenate(
                        [side[:BLK // 2], side[BLK // 2:]], axis=1
                    )

    core = head % 2

    def peer_at(index):
        turned = (index + core) % others
        odd = turned % 2
        return (1 - odd) * (seq_count // 2 + turned // 2) + odd * ((turned + 1) // 2) - 1

    @pl.loop(0, others)
    def _(index):
        step = peer_at(index)
        gather(0, step)
        far_copy(0, step).start()

    for g in range(1, kv_local):
        @pl.loop(0, others)
        def _(step):
            gather(g, step)

    def advance(g):
        @pl.loop(0, others)
        def _(index):
            step = peer_at(index)
            far_copy(g, step).wait_send()
            far_copy(g + 1, step).start()

    q_own.wait()
    for step in range(1, head_count):
        q_copy(step).wait_recv()

    pair = 2 if ratio % 2 == 0 else 1
    scale = HD ** -0.5 * LOG2E

    def query_parts(g, b):
        q_rows = q_buf[aligned(b, BLK), g * width:(g + 1) * width]
        for first in range(0, ratio, pair):
            yield first, jnp.concatenate(
                [q_rows[:, r * HD:(r + 1) * HD] for r in range(first, first + pair)], axis=0
            )

    def scores_of(q_part, k_all):
        return lax.dot_general(
            q_part, k_all, (((1,), (1,)), ((), ())), preferred_element_type=jnp.float32
        )

    def near_part(g, b):
        columns = slice(g * HD, (g + 1) * HD)
        near = [lax.rem(ids[j, b], k_buf.shape[0]) for j in range(NEAR)]
        k_all = jnp.concatenate([k_buf[block, :, columns] for block in near], axis=0)
        v_all = jnp.concatenate([v_buf[block, :, columns] for block in near], axis=0)
        for first, q_part in query_parts(g, b):
            scores = scores_of(q_part, k_all)
            highest = jnp.max(scores, axis=1, keepdims=True)
            exponent = jnp.exp2((scores - highest) * scale)
            total = jnp.sum(exponent, axis=1, keepdims=True)
            mixed = jnp.dot(
                exponent.astype(jnp.bfloat16), v_all, preferred_element_type=jnp.float32
            )
            rows_of = pl.ds(first * BLK, pair * BLK)
            near_mixed[b, rows_of, :] = mixed
            near_high[b, rows_of, :] = jnp.broadcast_to(highest, mixed.shape)
            near_total[b, rows_of, :] = jnp.broadcast_to(total, mixed.shape)

    def far_part(g, b):
        far = [slots_of[j, b] for j in range(far_count)]
        k_all = jnp.concatenate([recv_bufs[g][block, :, 0:HD] for block in far], axis=0)
        v_all = jnp.concatenate([recv_bufs[g][block, :, HD:] for block in far], axis=0)
        for first, q_part in query_parts(g, b):
            rows_of = pl.ds(first * BLK, pair * BLK)
            scores = scores_of(q_part, k_all)
            before = near_high[b, rows_of, :]
            highest = jnp.maximum(before, jnp.max(scores, axis=1, keepdims=True))
            factor = jnp.exp2((before - highest) * scale)
            exponent = jnp.concatenate(
                [
                    jnp.exp2((scores[:, j * BLK:(j + 1) * BLK] - highest) * scale)
                    for j in range(far_count)
                ],
                axis=1,
            )
            total = near_total[b, rows_of, :] * factor + jnp.sum(exponent, axis=1, keepdims=True)
            mixed = near_mixed[b, rows_of, :] * factor + jnp.dot(
                exponent.astype(jnp.bfloat16), v_all, preferred_element_type=jnp.float32
            )
            result = (mixed / total).astype(jnp.bfloat16)
            for r in range(pair):
                stages[g][b, :, (first + r) * HD:(first + r + 1) * HD] = (
                    result[r * BLK:(r + 1) * BLK]
                )

    def weigh_part(b):
        far = [slots_of[j, b] for j in range(far_count)]
        k_all = jnp.concatenate([recv_bufs[last][block] for block in far], axis=0)
        for first, q_part in query_parts(last, b):
            rows_of = pl.ds(first * BLK, pair * BLK)
            scores = scores_of(q_part, k_all)
            before = near_high[b, rows_of, :]
            highest = jnp.maximum(before, jnp.max(scores, axis=1, keepdims=True))
            factor = jnp.exp2((before - highest) * scale)
            exponent = jnp.concatenate(
                [
                    jnp.exp2((scores[:, j * BLK:(j + 1) * BLK] - highest) * scale)
                    for j in range(far_count)
                ],
                axis=1,
            )
            total = near_total[b, rows_of, :] * factor + jnp.sum(exponent, axis=1, keepdims=True)
            near_total[b, rows_of, :] = 1.0 / total
            near_mixed[b, rows_of, :] = near_mixed[b, rows_of, :] * factor
            far_weight[b, rows_of, :] = exponent.astype(jnp.bfloat16)

    def blend_part(part, b):
        far = [slots_of[j, b] for j in range(far_count)]
        sides = []
        for block in far:
            packed = recv_bufs[last + 1 + part][block]
            sides += [packed[:, :half], packed[:, half:]]
        v_all = jnp.concatenate(sides, axis=0)
        pieces = []
        for first in range(0, ratio, pair):
            rows_of = pl.ds(first * BLK, pair * BLK)
            mixed = near_mixed[b, rows_of, part * half:(part + 1) * half] + jnp.dot(
                far_weight[b, rows_of, :], v_all, preferred_element_type=jnp.float32
            )
            result = (mixed * near_total[b, rows_of, 0:half]).astype(jnp.bfloat16)
            pieces += [result[r * BLK:(r + 1) * BLK] for r in range(pair)]
        stages[last + part][b] = jnp.concatenate(pieces, axis=1)

    def arrive(piece):
        @pl.loop(0, others)
        def _(step):
            far_copy(piece, step).wait_recv()

    def hand_out(part, finish):
        @pl.loop(0, (head_count - 1) * per_head)
        def _(index):
            step = head_count - 1 - index // per_head
            j = index % per_head
            finish(head_peer(step) * per_head + j)
            out_copy(part, step, j).start()

        @pl.loop(0, per_head)
        def _(j):
            finish(head * per_head + j)
            own_copy(part, j).start()

    for g in range(kv_local):
        @pl.loop(0, head_count * per_head)
        def _(b):
            near_part(g, b)

        advance(g)
        arrive(g)
        if g < last:
            hand_out(g, functools.partial(far_part, g))

    @pl.loop(0, head_count * per_head)
    def _(b):
        weigh_part(b)

    advance(last + 1)
    arrive(last + 1)
    hand_out(last, functools.partial(blend_part, 0))
    arrive(last + 2)
    hand_out(last + 1, functools.partial(blend_part, 1))

    for step in range(others):
        id_copy(step).wait_send()
        far_copy(last + 2, step).wait_send()
    for step in range(1, head_count):
        q_copy(step).wait_send()
    for part in range(kv_local + 1):
        @pl.loop(0, (head_count - 1) * per_head)
        def _(index):
            step = head_count - 1 - index // per_head
            j = index % per_head
            out_copy(part, step, j).wait()

        @pl.loop(0, per_head)
        def _(j):
            own_copy(part, j).wait()


def side_by_side(head_count, ratio, whole_count, *refs):
    *wholes, left, right, out = refs
    half = HD // 2
    width = ratio * HD
    for head in range(head_count):
        start = head * (whole_count + 1) * width
        for g in range(whole_count):
            out[:, start + g * width:start + (g + 1) * width] = (
                wholes[g][:, head * width:(head + 1) * width]
            )
        start += whole_count * width
        for r in range(ratio):
            column = (head * ratio + r) * half
            out[:, start + r * HD:start + (r + 1) * HD] = jnp.concatenate(
                [left[:, column:column + half], right[:, column:column + half]], axis=1
            )


def shards(queries, cache_keys, cache_values, block_ids):
    seq_count = lax.axis_size("seq")
    head_count = lax.axis_size("head")
    seq = lax.axis_index("seq")
    rows, q_columns = queries.shape
    q_width = q_columns // head_count
    kv_local = cache_keys.shape[1] // HD
    ratio = q_width // (kv_local * HD)
    q_count, picks = block_ids.shape
    per_head = q_count // head_count
    k_count = cache_keys.shape[0] // BLK
    far_count = picks - NEAR
    others = seq_count - 1
    capacity = max(2, (far_count * q_count + seq_count - 2) // others)

    ids = block_ids.T
    far = ids[NEAR:].reshape(-1)
    owner = far // k_count
    within = far - owner * k_count
    distance = (seq ^ owner) - 1
    order = jnp.arange(far.shape[0], dtype=jnp.int32)
    earlier = (distance[:, None] == distance[None, :]) & (order[None, :] < order[:, None])
    rank = jnp.sum(earlier.astype(jnp.int32), axis=1)
    slot = distance * capacity + rank
    slots_of = slot.reshape(far_count, q_count)
    lane = jnp.arange(128, dtype=jnp.int32)[None, None, None, :]
    shape = (far.shape[0], others, 8, 128)
    hit = (
        (distance[:, None, None, None] == jnp.arange(others, dtype=jnp.int32)[None, :, None, None])
        & (rank[:, None, None, None] == lane)
    )
    asked = jnp.sum(
        jnp.where(jnp.broadcast_to(hit, shape), within[:, None, None, None], 0), axis=0
    )

    slots = others * capacity
    blocks = (k_count, BLK, cache_keys.shape[1])
    bf16 = jnp.bfloat16
    width = ratio * HD
    spans = [width] * (kv_local - 1) + [width // 2] * 2
    pieces = [(slots, BLK, 2 * HD)] * (kv_local - 1)
    pieces += [(slots, BLK, HD)] + [(slots, BLK // 2, HD)] * 2
    dma = pltpu.SemaphoreType.DMA
    anywhere = pl.BlockSpec(memory_space=pl.ANY)
    landed = pl.pallas_call(
        functools.partial(
            kernel, seq_count, head_count, capacity, kv_local, ratio, per_head, far_count
        ),
        out_shape=[jax.ShapeDtypeStruct((rows, head_count * span), bf16) for span in spans],
        in_specs=[
            pl.BlockSpec(memory_space=pltpu.SMEM),
            pl.BlockSpec(memory_space=pltpu.SMEM),
            pl.BlockSpec(memory_space=pltpu.VMEM),
            anywhere, anywhere, anywhere,
        ],
        out_specs=[anywhere for _ in spans],
        scratch_shapes=[
            pltpu.VMEM(blocks, bf16),
            pltpu.VMEM(blocks, bf16),
            pltpu.VMEM((rows * head_count, q_width), bf16),
            pltpu.VMEM((others, 8, 128), jnp.int32),
            pltpu.SMEM((others, 8, 128), jnp.int32),
            [pltpu.VMEM(piece, bf16) for piece in pieces],
            [pltpu.VMEM(piece, bf16) for piece in pieces],
            [pltpu.VMEM((q_count, BLK, span), bf16) for span in spans],
            dma((others,)), dma((others,)),
            dma((head_count - 1,)), dma((head_count - 1,)),
            dma((len(pieces), others)), dma((len(pieces), others)),
            dma((len(spans), head_count - 1, per_head)),
            dma((len(spans), head_count - 1, per_head)),
            dma((len(spans), per_head)),
            dma((4,)),
            pltpu.VMEM((q_count, ratio * BLK, HD), jnp.float32),
            pltpu.VMEM((q_count, ratio * BLK, HD), jnp.float32),
            pltpu.VMEM((q_count, ratio * BLK, HD), jnp.float32),
            pltpu.VMEM((q_count, ratio * BLK, far_count * BLK), bf16),
        ],
        compiler_params=pltpu.CompilerParams(
            collective_id=0, has_side_effects=True, vmem_limit_bytes=56 * 2**20
        ),
    )(ids, slots_of, asked, queries, cache_keys.reshape(blocks), cache_values.reshape(blocks))
    return pl.pallas_call(
        functools.partial(side_by_side, head_count, ratio, kv_local - 1),
        grid=(rows // TILE,),
        out_shape=jax.ShapeDtypeStruct((rows, q_columns), bf16),
        in_specs=[pl.BlockSpec((TILE, head_count * span), lambda i: (i, 0)) for span in spans],
        out_specs=pl.BlockSpec((TILE, q_columns), lambda i: (i, 0)),
        compiler_params=pltpu.CompilerParams(vmem_limit_bytes=62 * 2**20),
    )(*landed)


def solution(mesh):
    return jax.shard_map(
        shards,
        mesh=mesh,
        in_specs=(P(("seq", "head"), None), P("seq", "head"), P("seq", "head"), P("seq", None)),
        out_specs=P(("seq", "head"), None),
        check_vma=False,
    )
```

```python
import functools
import math

import jax
import jax.numpy as jnp
from jax import lax
from jax.experimental import pallas as pl
from jax.experimental.pallas import tpu as pltpu
from jax.sharding import PartitionSpec as P

HD = 128
BLK = 128
NEAR = 5
TILE = 64
CHUNKS = 2
MESH = pl.DeviceIdType.MESH
LOG2E = math.log2(math.e)


def aligned(index, size):
    return pl.ds(pl.multiple_of(index * size, size), size)


def kernel(
    seq_count, head_count, capacity, kv_local, ratio, per_head, far_count,
    ids, slots_of, asked, queries, keys, values, *rest
):
    landed, rest = rest[:kv_local + 1], rest[kv_local + 1:]
    (
        k_buf, v_buf, q_buf, got, wanted, send_bufs, recv_bufs, stages,
        id_send, id_recv, q_send, q_recv, f_send, f_recv, o_send, o_recv, o_local, local,
        near_mixed, near_high, near_total, far_weight,
    ) = rest
    seq = lax.axis_index("seq")
    head = lax.axis_index("head")
    others = seq_count - 1
    rows = queries.shape[0]
    q_width = q_buf.shape[1]
    width = ratio * HD
    last = kv_local - 1
    half = HD // 2

    def seq_peer(step):
        peer = 0
        weight = 1
        while weight < seq_count:
            peer += (seq // weight + (step + 1) // weight) % 2 * weight
            weight *= 2
        return peer

    def head_peer(step):
        return (head // 2 + step // 2) % 2 * 2 + (head % 2 + step % 2) % 2

    k_load = pltpu.make_async_copy(keys, k_buf, local.at[0])
    v_load = pltpu.make_async_copy(values, v_buf, local.at[1])
    q_own = pltpu.make_async_copy(
        queries.at[:, aligned(head, q_width)], q_buf.at[aligned(head, rows)], local.at[2]
    )
    k_load.start()
    v_load.start()
    q_own.start()

    barrier = pltpu.get_barrier_semaphore()
    for step in range(others):
        pl.semaphore_signal(
            barrier, inc=1, device_id={"seq": seq_peer(step)}, device_id_type=MESH
        )
    for step in range(1, head_count):
        pl.semaphore_signal(
            barrier, inc=1, device_id={"head": head_peer(step)}, device_id_type=MESH
        )
    pl.semaphore_wait(barrier, others + head_count - 1)

    def id_copy(step):
        return pltpu.make_async_remote_copy(
            src_ref=asked.at[step],
            dst_ref=got.at[step],
            send_sem=id_send.at[step],
            recv_sem=id_recv.at[step],
            device_id={"seq": seq_peer(step)},
            device_id_type=MESH,
        )

    def q_copy(step):
        peer = head_peer(step)
        return pltpu.make_async_remote_copy(
            src_ref=queries.at[:, aligned(peer, q_width)],
            dst_ref=q_buf.at[aligned(head, rows)],
            send_sem=q_send.at[step - 1],
            recv_sem=q_recv.at[step - 1],
            device_id={"head": peer},
            device_id_type=MESH,
        )

    chunk = capacity // CHUNKS

    def far_copy(g, part, step):
        block = pl.ds(step * capacity + part * chunk, chunk)
        return pltpu.make_async_remote_copy(
            src_ref=send_bufs[g].at[block],
            dst_ref=recv_bufs[g].at[block],
            send_sem=f_send.at[g, part, step],
            recv_sem=f_recv.at[g, part, step],
            device_id={"seq": seq_peer(step)},
            device_id_type=MESH,
        )

    def place(part, j):
        span = stages[part].shape[2]
        return landed[part].at[aligned(j, BLK), aligned(head, span)]

    def out_copy(part, step, j):
        peer = head_peer(step)
        return pltpu.make_async_remote_copy(
            src_ref=stages[part].at[peer * per_head + j],
            dst_ref=place(part, j),
            send_sem=o_send.at[part, step - 1, j],
            recv_sem=o_recv.at[part, step - 1, j],
            device_id={"head": peer},
            device_id_type=MESH,
        )

    def own_copy(part, j):
        return pltpu.make_async_copy(
            stages[part].at[head * per_head + j], place(part, j), o_local.at[part, j]
        )

    for step in range(others):
        id_copy(step).start()
    for step in range(head_count - 1, 0, -1):
        q_copy(step).start()
    for step in range(others):
        id_copy(step).wait_recv()
    to_scalar = pltpu.make_async_copy(got, wanted, local.at[3])
    to_scalar.start()
    to_scalar.wait()
    k_load.wait()
    v_load.wait()

    def gather(g, step):
        columns = slice(g * HD, (g + 1) * HD)
        for slot in range(capacity):
            block = wanted[step, 0, slot]
            spot = step * capacity + slot
            if g < last:
                send_bufs[g][spot, :, 0:HD] = k_buf[block, :, columns]
                send_bufs[g][spot, :, HD:] = v_buf[block, :, columns]
            else:
                send_bufs[g][spot] = k_buf[block, :, columns]
                value = v_buf[block, :, columns]
                for part in range(2):
                    side = value[:, part * half:(part + 1) * half]
                    send_bufs[g + 1 + part][spot] = jnp.concatenate(
                        [side[:BLK // 2], side[BLK // 2:]], axis=1
                    )

    core = head % 2

    def peer_at(index):
        turned = (index + core) % others
        odd = turned % 2
        return (1 - odd) * (seq_count // 2 + turned // 2) + odd * ((turned + 1) // 2) - 1

    @pl.loop(0, others)
    def _(index):
        step = peer_at(index)
        gather(0, step)
        far_copy(0, 0, step).start()

    for part in range(1, CHUNKS):
        @pl.loop(0, others)
        def _(index):
            far_copy(0, part, peer_at(index)).start()

    for g in range(1, kv_local):
        @pl.loop(0, others)
        def _(step):
            gather(g, step)

    def advance(g, part):
        @pl.loop(0, others)
        def _(index):
            step = peer_at(index)
            far_copy(g, part, step).wait_send()
            far_copy(g + 1, part, step).start()

    q_own.wait()
    for step in range(1, head_count):
        q_copy(step).wait_recv()

    pair = 2 if ratio % 2 == 0 else 1
    scale = HD ** -0.5 * LOG2E

    def query_parts(g, b):
        q_rows = q_buf[aligned(b, BLK), g * width:(g + 1) * width]
        for first in range(0, ratio, pair):
            yield first, jnp.concatenate(
                [q_rows[:, r * HD:(r + 1) * HD] for r in range(first, first + pair)], axis=0
            )

    def scores_of(q_part, k_all):
        return lax.dot_general(
            q_part, k_all, (((1,), (1,)), ((), ())), preferred_element_type=jnp.float32
        )

    def near_part(g, b):
        columns = slice(g * HD, (g + 1) * HD)
        near = [lax.rem(ids[j, b], k_buf.shape[0]) for j in range(NEAR)]
        k_all = jnp.concatenate([k_buf[block, :, columns] for block in near], axis=0)
        v_all = jnp.concatenate([v_buf[block, :, columns] for block in near], axis=0)
        for first, q_part in query_parts(g, b):
            scores = scores_of(q_part, k_all)
            highest = jnp.max(scores, axis=1, keepdims=True)
            exponent = jnp.exp2((scores - highest) * scale)
            total = jnp.sum(exponent, axis=1, keepdims=True)
            mixed = jnp.dot(
                exponent.astype(jnp.bfloat16), v_all, preferred_element_type=jnp.float32
            )
            rows_of = pl.ds(first * BLK, pair * BLK)
            near_mixed[b, rows_of, :] = mixed
            near_high[b, rows_of, :] = jnp.broadcast_to(highest, mixed.shape)
            near_total[b, rows_of, :] = jnp.broadcast_to(total, mixed.shape)

    def far_part(g, b):
        far = [slots_of[j, b] for j in range(far_count)]
        k_all = jnp.concatenate([recv_bufs[g][block, :, 0:HD] for block in far], axis=0)
        v_all = jnp.concatenate([recv_bufs[g][block, :, HD:] for block in far], axis=0)
        for first, q_part in query_parts(g, b):
            rows_of = pl.ds(first * BLK, pair * BLK)
            scores = scores_of(q_part, k_all)
            before = near_high[b, rows_of, :]
            highest = jnp.maximum(before, jnp.max(scores, axis=1, keepdims=True))
            factor = jnp.exp2((before - highest) * scale)
            exponent = jnp.concatenate(
                [
                    jnp.exp2((scores[:, j * BLK:(j + 1) * BLK] - highest) * scale)
                    for j in range(far_count)
                ],
                axis=1,
            )
            total = near_total[b, rows_of, :] * factor + jnp.sum(exponent, axis=1, keepdims=True)
            mixed = near_mixed[b, rows_of, :] * factor + jnp.dot(
                exponent.astype(jnp.bfloat16), v_all, preferred_element_type=jnp.float32
            )
            result = (mixed / total).astype(jnp.bfloat16)
            for r in range(pair):
                stages[g][b, :, (first + r) * HD:(first + r + 1) * HD] = (
                    result[r * BLK:(r + 1) * BLK]
                )

    def weigh_part(b):
        far = [slots_of[j, b] for j in range(far_count)]
        k_all = jnp.concatenate([recv_bufs[last][block] for block in far], axis=0)
        for first, q_part in query_parts(last, b):
            rows_of = pl.ds(first * BLK, pair * BLK)
            scores = scores_of(q_part, k_all)
            before = near_high[b, rows_of, :]
            highest = jnp.maximum(before, jnp.max(scores, axis=1, keepdims=True))
            factor = jnp.exp2((before - highest) * scale)
            exponent = jnp.concatenate(
                [
                    jnp.exp2((scores[:, j * BLK:(j + 1) * BLK] - highest) * scale)
                    for j in range(far_count)
                ],
                axis=1,
            )
            total = near_total[b, rows_of, :] * factor + jnp.sum(exponent, axis=1, keepdims=True)
            near_total[b, rows_of, :] = 1.0 / total
            near_mixed[b, rows_of, :] = near_mixed[b, rows_of, :] * factor
            far_weight[b, rows_of, :] = exponent.astype(jnp.bfloat16)

    def blend_part(part, b):
        far = [slots_of[j, b] for j in range(far_count)]
        sides = []
        for block in far:
            packed = recv_bufs[last + 1 + part][block]
            sides += [packed[:, :half], packed[:, half:]]
        v_all = jnp.concatenate(sides, axis=0)
        pieces = []
        for first in range(0, ratio, pair):
            rows_of = pl.ds(first * BLK, pair * BLK)
            mixed = near_mixed[b, rows_of, part * half:(part + 1) * half] + jnp.dot(
                far_weight[b, rows_of, :], v_all, preferred_element_type=jnp.float32
            )
            result = (mixed * near_total[b, rows_of, 0:half]).astype(jnp.bfloat16)
            pieces += [result[r * BLK:(r + 1) * BLK] for r in range(pair)]
        stages[last + part][b] = jnp.concatenate(pieces, axis=1)

    def arrive(piece):
        @pl.loop(0, others)
        def _(step):
            for part in range(CHUNKS):
                far_copy(piece, part, step).wait_recv()

    def hand_out(part, finish):
        @pl.loop(0, (head_count - 1) * per_head)
        def _(index):
            step = head_count - 1 - index // per_head
            j = index % per_head
            finish(head_peer(step) * per_head + j)
            out_copy(part, step, j).start()

        @pl.loop(0, per_head)
        def _(j):
            finish(head * per_head + j)
            own_copy(part, j).start()

    for g in range(kv_local):
        for part in range(CHUNKS - 1):
            if g == 0:
                advance(g, part)

        @pl.loop(0, head_count * per_head)
        def _(b):
            near_part(g, b)

        for part in range(CHUNKS - 1):
            if g > 0:
                advance(g, part)
        advance(g, CHUNKS - 1)
        arrive(g)
        if g < last:
            hand_out(g, functools.partial(far_part, g))

    @pl.loop(0, head_count * per_head)
    def _(b):
        weigh_part(b)

    for part in range(CHUNKS):
        advance(last + 1, part)
    arrive(last + 1)
    hand_out(last, functools.partial(blend_part, 0))
    arrive(last + 2)
    hand_out(last + 1, functools.partial(blend_part, 1))

    for step in range(others):
        id_copy(step).wait_send()
        for part in range(CHUNKS):
            far_copy(last + 2, part, step).wait_send()
    for step in range(1, head_count):
        q_copy(step).wait_send()
    for part in range(kv_local + 1):
        @pl.loop(0, (head_count - 1) * per_head)
        def _(index):
            step = head_count - 1 - index // per_head
            j = index % per_head
            out_copy(part, step, j).wait()

        @pl.loop(0, per_head)
        def _(j):
            own_copy(part, j).wait()


def side_by_side(head_count, ratio, whole_count, *refs):
    *wholes, left, right, out = refs
    half = HD // 2
    width = ratio * HD
    for head in range(head_count):
        start = head * (whole_count + 1) * width
        for g in range(whole_count):
            out[:, start + g * width:start + (g + 1) * width] = (
                wholes[g][:, head * width:(head + 1) * width]
            )
        start += whole_count * width
        for r in range(ratio):
            column = (head * ratio + r) * half
            out[:, start + r * HD:start + (r + 1) * HD] = jnp.concatenate(
                [left[:, column:column + half], right[:, column:column + half]], axis=1
            )


def shards(queries, cache_keys, cache_values, block_ids):
    seq_count = lax.axis_size("seq")
    head_count = lax.axis_size("head")
    seq = lax.axis_index("seq")
    rows, q_columns = queries.shape
    q_width = q_columns // head_count
    kv_local = cache_keys.shape[1] // HD
    ratio = q_width // (kv_local * HD)
    q_count, picks = block_ids.shape
    per_head = q_count // head_count
    k_count = cache_keys.shape[0] // BLK
    far_count = picks - NEAR
    others = seq_count - 1
    capacity = max(2, (far_count * q_count + seq_count - 2) // others)
    capacity += -capacity % CHUNKS

    ids = block_ids.T
    far = ids[NEAR:].reshape(-1)
    owner = far // k_count
    within = far - owner * k_count
    distance = (seq ^ owner) - 1
    order = jnp.arange(far.shape[0], dtype=jnp.int32)
    earlier = (distance[:, None] == distance[None, :]) & (order[None, :] < order[:, None])
    rank = jnp.sum(earlier.astype(jnp.int32), axis=1)
    slot = distance * capacity + rank
    slots_of = slot.reshape(far_count, q_count)
    lane = jnp.arange(128, dtype=jnp.int32)[None, None, None, :]
    shape = (far.shape[0], others, 8, 128)
    hit = (
        (distance[:, None, None, None] == jnp.arange(others, dtype=jnp.int32)[None, :, None, None])
        & (rank[:, None, None, None] == lane)
    )
    asked = jnp.sum(
        jnp.where(jnp.broadcast_to(hit, shape), within[:, None, None, None], 0), axis=0
    )

    slots = others * capacity
    blocks = (k_count, BLK, cache_keys.shape[1])
    bf16 = jnp.bfloat16
    width = ratio * HD
    spans = [width] * (kv_local - 1) + [width // 2] * 2
    pieces = [(slots, BLK, 2 * HD)] * (kv_local - 1)
    pieces += [(slots, BLK, HD)] + [(slots, BLK // 2, HD)] * 2
    dma = pltpu.SemaphoreType.DMA
    anywhere = pl.BlockSpec(memory_space=pl.ANY)
    landed = pl.pallas_call(
        functools.partial(
            kernel, seq_count, head_count, capacity, kv_local, ratio, per_head, far_count
        ),
        out_shape=[jax.ShapeDtypeStruct((rows, head_count * span), bf16) for span in spans],
        in_specs=[
            pl.BlockSpec(memory_space=pltpu.SMEM),
            pl.BlockSpec(memory_space=pltpu.SMEM),
            pl.BlockSpec(memory_space=pltpu.VMEM),
            anywhere, anywhere, anywhere,
        ],
        out_specs=[anywhere for _ in spans],
        scratch_shapes=[
            pltpu.VMEM(blocks, bf16),
            pltpu.VMEM(blocks, bf16),
            pltpu.VMEM((rows * head_count, q_width), bf16),
            pltpu.VMEM((others, 8, 128), jnp.int32),
            pltpu.SMEM((others, 8, 128), jnp.int32),
            [pltpu.VMEM(piece, bf16) for piece in pieces],
            [pltpu.VMEM(piece, bf16) for piece in pieces],
            [pltpu.VMEM((q_count, BLK, span), bf16) for span in spans],
            dma((others,)), dma((others,)),
            dma((head_count - 1,)), dma((head_count - 1,)),
            dma((len(pieces), CHUNKS, others)), dma((len(pieces), CHUNKS, others)),
            dma((len(spans), head_count - 1, per_head)),
            dma((len(spans), head_count - 1, per_head)),
            dma((len(spans), per_head)),
            dma((4,)),
            pltpu.VMEM((q_count, ratio * BLK, HD), jnp.float32),
            pltpu.VMEM((q_count, ratio * BLK, HD), jnp.float32),
            pltpu.VMEM((q_count, ratio * BLK, HD), jnp.float32),
            pltpu.VMEM((q_count, ratio * BLK, far_count * BLK), bf16),
        ],
        compiler_params=pltpu.CompilerParams(
            collective_id=0, has_side_effects=True, vmem_limit_bytes=50 * 2**20
        ),
    )(ids, slots_of, asked, queries, cache_keys.reshape(blocks), cache_values.reshape(blocks))
    return pl.pallas_call(
        functools.partial(side_by_side, head_count, ratio, kv_local - 1),
        grid=(rows // TILE,),
        out_shape=jax.ShapeDtypeStruct((rows, q_columns), bf16),
        in_specs=[pl.BlockSpec((TILE, head_count * span), lambda i: (i, 0)) for span in spans],
        out_specs=pl.BlockSpec((TILE, q_columns), lambda i: (i, 0)),
    )(*landed)


def solution(mesh):
    return jax.shard_map(
        shards,
        mesh=mesh,
        in_specs=(P(("seq", "head"), None), P("seq", "head"), P("seq", "head"), P("seq", None)),
        out_specs=P(("seq", "head"), None),
        check_vma=False,
    )
```

```python
import functools
import math

import jax
import jax.numpy as jnp
from jax import lax
from jax.experimental import pallas as pl
from jax.experimental.pallas import tpu as pltpu
from jax.sharding import PartitionSpec as P

HD = 128
BLK = 128
NEAR = 5
TILE = 64
CHUNKS = 2
MESH = pl.DeviceIdType.MESH
LOG2E = math.log2(math.e)


def aligned(index, size):
    return pl.ds(pl.multiple_of(index * size, size), size)


def kernel(
    seq_count, head_count, capacity, kv_local, ratio, per_head, far_count,
    ids, slots_of, asked, queries, keys, values, *rest
):
    landed, rest = rest[:kv_local + 1], rest[kv_local + 1:]
    (
        k_buf, v_buf, q_buf, got, wanted, send_bufs, recv_bufs, stages,
        id_send, id_recv, q_send, q_recv, f_send, f_recv, o_send, o_recv, o_local, local,
        near_mixed, near_high, near_total, far_weight,
    ) = rest
    seq = lax.axis_index("seq")
    head = lax.axis_index("head")
    others = seq_count - 1
    rows = queries.shape[0]
    q_width = q_buf.shape[1]
    width = ratio * HD
    last = kv_local - 1
    half = HD // 2

    def seq_peer(step):
        peer = 0
        weight = 1
        while weight < seq_count:
            peer += (seq // weight + (step + 1) // weight) % 2 * weight
            weight *= 2
        return peer

    def head_peer(step):
        return (head // 2 + step // 2) % 2 * 2 + (head % 2 + step % 2) % 2

    k_load = pltpu.make_async_copy(keys, k_buf, local.at[0])
    v_load = pltpu.make_async_copy(values, v_buf, local.at[1])
    q_own = pltpu.make_async_copy(
        queries.at[:, aligned(head, q_width)], q_buf.at[aligned(head, rows)], local.at[2]
    )
    k_load.start()
    v_load.start()
    q_own.start()

    barrier = pltpu.get_barrier_semaphore()
    for step in range(others):
        pl.semaphore_signal(
            barrier, inc=1, device_id={"seq": seq_peer(step)}, device_id_type=MESH
        )
    for step in range(1, head_count):
        pl.semaphore_signal(
            barrier, inc=1, device_id={"head": head_peer(step)}, device_id_type=MESH
        )
    pl.semaphore_wait(barrier, others + head_count - 1)

    def id_copy(step):
        return pltpu.make_async_remote_copy(
            src_ref=asked.at[step],
            dst_ref=got.at[step],
            send_sem=id_send.at[step],
            recv_sem=id_recv.at[step],
            device_id={"seq": seq_peer(step)},
            device_id_type=MESH,
        )

    def q_copy(step):
        peer = head_peer(step)
        return pltpu.make_async_remote_copy(
            src_ref=queries.at[:, aligned(peer, q_width)],
            dst_ref=q_buf.at[aligned(head, rows)],
            send_sem=q_send.at[step - 1],
            recv_sem=q_recv.at[step - 1],
            device_id={"head": peer},
            device_id_type=MESH,
        )

    chunk = capacity // CHUNKS

    def far_copy(g, part, step):
        block = pl.ds(step * capacity + part * chunk, chunk)
        return pltpu.make_async_remote_copy(
            src_ref=send_bufs[g].at[block],
            dst_ref=recv_bufs[g].at[block],
            send_sem=f_send.at[g, part, step],
            recv_sem=f_recv.at[g, part, step],
            device_id={"seq": seq_peer(step)},
            device_id_type=MESH,
        )

    def place(part, j):
        span = stages[part].shape[2]
        return landed[part].at[aligned(j, BLK), aligned(head, span)]

    def out_copy(part, step, j):
        peer = head_peer(step)
        return pltpu.make_async_remote_copy(
            src_ref=stages[part].at[peer * per_head + j],
            dst_ref=place(part, j),
            send_sem=o_send.at[part, step - 1, j],
            recv_sem=o_recv.at[part, step - 1, j],
            device_id={"head": peer},
            device_id_type=MESH,
        )

    def own_copy(part, j):
        return pltpu.make_async_copy(
            stages[part].at[head * per_head + j], place(part, j), o_local.at[part, j]
        )

    for step in range(others):
        id_copy(step).start()
    for step in range(head_count - 1, 0, -1):
        q_copy(step).start()
    for step in range(others):
        id_copy(step).wait_recv()
    to_scalar = pltpu.make_async_copy(got, wanted, local.at[3])
    to_scalar.start()
    to_scalar.wait()
    k_load.wait()
    v_load.wait()

    def gather(g, step):
        columns = slice(g * HD, (g + 1) * HD)
        for slot in range(capacity):
            block = wanted[step, 0, slot]
            spot = step * capacity + slot
            if g < last:
                send_bufs[g][spot, :, 0:HD] = k_buf[block, :, columns]
                send_bufs[g][spot, :, HD:] = v_buf[block, :, columns]
            else:
                send_bufs[g][spot] = k_buf[block, :, columns]
                value = v_buf[block, :, columns]
                for part in range(2):
                    side = value[:, part * half:(part + 1) * half]
                    send_bufs[g + 1 + part][spot] = jnp.concatenate(
                        [side[:BLK // 2], side[BLK // 2:]], axis=1
                    )

    core = head % 2

    def peer_at(index):
        turned = (index + core) % others
        odd = turned % 2
        return (1 - odd) * (seq_count // 2 + turned // 2) + odd * ((turned + 1) // 2) - 1

    @pl.loop(0, others)
    def _(index):
        step = peer_at(index)
        gather(0, step)
        far_copy(0, 0, step).start()

    for part in range(1, CHUNKS):
        @pl.loop(0, others)
        def _(index):
            far_copy(0, part, peer_at(index)).start()

    for g in range(1, kv_local):
        @pl.loop(0, others)
        def _(step):
            gather(g, step)

    def advance(g, part):
        @pl.loop(0, others)
        def _(index):
            step = peer_at(index)
            far_copy(g, part, step).wait_send()
            far_copy(g + 1, part, step).start()

    q_own.wait()
    for step in range(1, head_count):
        q_copy(step).wait_recv()

    pair = 2 if ratio % 2 == 0 else 1
    scale = HD ** -0.5 * LOG2E

    def query_parts(g, b):
        q_rows = q_buf[aligned(b, BLK), g * width:(g + 1) * width]
        for first in range(0, ratio, pair):
            yield first, jnp.concatenate(
                [q_rows[:, r * HD:(r + 1) * HD] for r in range(first, first + pair)], axis=0
            )

    def scores_of(q_part, k_all):
        return lax.dot_general(
            q_part, k_all, (((1,), (1,)), ((), ())), preferred_element_type=jnp.float32
        )

    def near_part(g, b):
        columns = slice(g * HD, (g + 1) * HD)
        near = [lax.rem(ids[j, b], k_buf.shape[0]) for j in range(NEAR)]
        k_all = jnp.concatenate([k_buf[block, :, columns] for block in near], axis=0)
        v_all = jnp.concatenate([v_buf[block, :, columns] for block in near], axis=0)
        for first, q_part in query_parts(g, b):
            scores = scores_of(q_part, k_all)
            highest = jnp.max(scores, axis=1, keepdims=True)
            exponent = jnp.exp2((scores - highest) * scale)
            total = jnp.sum(exponent, axis=1, keepdims=True)
            mixed = jnp.dot(
                exponent.astype(jnp.bfloat16), v_all, preferred_element_type=jnp.float32
            )
            rows_of = pl.ds(first * BLK, pair * BLK)
            near_mixed[b, rows_of, :] = mixed
            near_high[b, rows_of, :] = jnp.broadcast_to(highest, mixed.shape)
            near_total[b, rows_of, :] = jnp.broadcast_to(total, mixed.shape)

    def far_part(g, b):
        far = [slots_of[j, b] for j in range(far_count)]
        k_all = jnp.concatenate([recv_bufs[g][block, :, 0:HD] for block in far], axis=0)
        v_all = jnp.concatenate([recv_bufs[g][block, :, HD:] for block in far], axis=0)
        for first, q_part in query_parts(g, b):
            rows_of = pl.ds(first * BLK, pair * BLK)
            scores = scores_of(q_part, k_all)
            before = near_high[b, rows_of, :]
            highest = jnp.maximum(before, jnp.max(scores, axis=1, keepdims=True))
            factor = jnp.exp2((before - highest) * scale)
            exponent = jnp.concatenate(
                [
                    jnp.exp2((scores[:, j * BLK:(j + 1) * BLK] - highest) * scale)
                    for j in range(far_count)
                ],
                axis=1,
            )
            total = near_total[b, rows_of, :] * factor + jnp.sum(exponent, axis=1, keepdims=True)
            mixed = near_mixed[b, rows_of, :] * factor + jnp.dot(
                exponent.astype(jnp.bfloat16), v_all, preferred_element_type=jnp.float32
            )
            result = (mixed / total).astype(jnp.bfloat16)
            for r in range(pair):
                stages[g][b, :, (first + r) * HD:(first + r + 1) * HD] = (
                    result[r * BLK:(r + 1) * BLK]
                )

    def weigh_part(b):
        far = [slots_of[j, b] for j in range(far_count)]
        k_all = jnp.concatenate([recv_bufs[last][block] for block in far], axis=0)
        for first, q_part in query_parts(last, b):
            rows_of = pl.ds(first * BLK, pair * BLK)
            scores = scores_of(q_part, k_all)
            before = near_high[b, rows_of, :]
            highest = jnp.maximum(before, jnp.max(scores, axis=1, keepdims=True))
            factor = jnp.exp2((before - highest) * scale)
            exponent = jnp.concatenate(
                [
                    jnp.exp2((scores[:, j * BLK:(j + 1) * BLK] - highest) * scale)
                    for j in range(far_count)
                ],
                axis=1,
            )
            total = near_total[b, rows_of, :] * factor + jnp.sum(exponent, axis=1, keepdims=True)
            near_total[b, rows_of, :] = 1.0 / total
            near_mixed[b, rows_of, :] = near_mixed[b, rows_of, :] * factor
            far_weight[b, rows_of, :] = exponent.astype(jnp.bfloat16)

    def blend_part(part, b):
        far = [slots_of[j, b] for j in range(far_count)]
        sides = []
        for block in far:
            packed = recv_bufs[last + 1 + part][block]
            sides += [packed[:, :half], packed[:, half:]]
        v_all = jnp.concatenate(sides, axis=0)
        pieces = []
        for first in range(0, ratio, pair):
            rows_of = pl.ds(first * BLK, pair * BLK)
            mixed = near_mixed[b, rows_of, part * half:(part + 1) * half] + jnp.dot(
                far_weight[b, rows_of, :], v_all, preferred_element_type=jnp.float32
            )
            result = (mixed * near_total[b, rows_of, 0:half]).astype(jnp.bfloat16)
            own = [result[r * BLK:(r + 1) * BLK] for r in range(pair)]
            pieces += own if part == 0 else own[::-1]
        stages[last + part][b] = jnp.concatenate(pieces, axis=1)

    def arrive(piece):
        @pl.loop(0, others)
        def _(step):
            for part in range(CHUNKS):
                far_copy(piece, part, step).wait_recv()

    def hand_out(part, finish):
        @pl.loop(0, (head_count - 1) * per_head)
        def _(index):
            step = head_count - 1 - index // per_head
            j = index % per_head
            finish(head_peer(step) * per_head + j)
            out_copy(part, step, j).start()

        @pl.loop(0, per_head)
        def _(j):
            finish(head * per_head + j)
            own_copy(part, j).start()

    for g in range(kv_local):
        for part in range(CHUNKS - 1):
            if g == 0:
                advance(g, part)

        @pl.loop(0, head_count * per_head)
        def _(b):
            near_part(g, b)

        for part in range(CHUNKS - 1):
            if g > 0:
                advance(g, part)
        advance(g, CHUNKS - 1)
        arrive(g)
        if g < last:
            hand_out(g, functools.partial(far_part, g))

    @pl.loop(0, head_count * per_head)
    def _(b):
        weigh_part(b)

    for part in range(CHUNKS):
        advance(last + 1, part)
    arrive(last + 1)
    hand_out(last, functools.partial(blend_part, 0))
    arrive(last + 2)
    hand_out(last + 1, functools.partial(blend_part, 1))

    for step in range(others):
        id_copy(step).wait_send()
        for part in range(CHUNKS):
            far_copy(last + 2, part, step).wait_send()
    for step in range(1, head_count):
        q_copy(step).wait_send()
    for part in range(kv_local + 1):
        @pl.loop(0, (head_count - 1) * per_head)
        def _(index):
            step = head_count - 1 - index // per_head
            j = index % per_head
            out_copy(part, step, j).wait()

        @pl.loop(0, per_head)
        def _(j):
            own_copy(part, j).wait()


def side_by_side(head_count, ratio, whole_count, *refs):
    *wholes, left, right, out = refs
    half = HD // 2
    width = ratio * HD
    for head in range(head_count):
        start = head * (whole_count + 1) * width
        for g in range(whole_count):
            out[:, start + g * width:start + (g + 1) * width] = (
                wholes[g][:, head * width:(head + 1) * width]
            )
        start += whole_count * width
        for r in range(0, ratio, 2):
            column = (head * ratio + r) * half
            first = left[:, column:column + HD].astype(jnp.float32)
            second = right[:, column:column + HD].astype(jnp.float32)
            low = lax.broadcasted_iota(jnp.int32, first.shape, 1) < half
            even = jnp.where(low, first, second)
            odd = pltpu.roll(jnp.where(low, second, first), half, 1)
            out[:, start + r * HD:start + (r + 1) * HD] = even.astype(out.dtype)
            out[:, start + (r + 1) * HD:start + (r + 2) * HD] = odd.astype(out.dtype)


def shards(queries, cache_keys, cache_values, block_ids):
    seq_count = lax.axis_size("seq")
    head_count = lax.axis_size("head")
    seq = lax.axis_index("seq")
    rows, q_columns = queries.shape
    q_width = q_columns // head_count
    kv_local = cache_keys.shape[1] // HD
    ratio = q_width // (kv_local * HD)
    q_count, picks = block_ids.shape
    per_head = q_count // head_count
    k_count = cache_keys.shape[0] // BLK
    far_count = picks - NEAR
    others = seq_count - 1
    capacity = max(2, (far_count * q_count + seq_count - 2) // others)
    capacity += -capacity % CHUNKS

    ids = block_ids.T
    far = ids[NEAR:].reshape(-1)
    owner = far // k_count
    within = far - owner * k_count
    distance = (seq ^ owner) - 1
    order = jnp.arange(far.shape[0], dtype=jnp.int32)
    earlier = (distance[:, None] == distance[None, :]) & (order[None, :] < order[:, None])
    rank = jnp.sum(earlier.astype(jnp.int32), axis=1)
    slot = distance * capacity + rank
    slots_of = slot.reshape(far_count, q_count)
    lane = jnp.arange(128, dtype=jnp.int32)[None, None, None, :]
    shape = (far.shape[0], others, 8, 128)
    hit = (
        (distance[:, None, None, None] == jnp.arange(others, dtype=jnp.int32)[None, :, None, None])
        & (rank[:, None, None, None] == lane)
    )
    asked = jnp.sum(
        jnp.where(jnp.broadcast_to(hit, shape), within[:, None, None, None], 0), axis=0
    )

    slots = others * capacity
    blocks = (k_count, BLK, cache_keys.shape[1])
    bf16 = jnp.bfloat16
    width = ratio * HD
    spans = [width] * (kv_local - 1) + [width // 2] * 2
    pieces = [(slots, BLK, 2 * HD)] * (kv_local - 1)
    pieces += [(slots, BLK, HD)] + [(slots, BLK // 2, HD)] * 2
    dma = pltpu.SemaphoreType.DMA
    anywhere = pl.BlockSpec(memory_space=pl.ANY)
    landed = pl.pallas_call(
        functools.partial(
            kernel, seq_count, head_count, capacity, kv_local, ratio, per_head, far_count
        ),
        out_shape=[jax.ShapeDtypeStruct((rows, head_count * span), bf16) for span in spans],
        in_specs=[
            pl.BlockSpec(memory_space=pltpu.SMEM),
            pl.BlockSpec(memory_space=pltpu.SMEM),
            pl.BlockSpec(memory_space=pltpu.VMEM),
            anywhere, anywhere, anywhere,
        ],
        out_specs=[anywhere for _ in spans],
        scratch_shapes=[
            pltpu.VMEM(blocks, bf16),
            pltpu.VMEM(blocks, bf16),
            pltpu.VMEM((rows * head_count, q_width), bf16),
            pltpu.VMEM((others, 8, 128), jnp.int32),
            pltpu.SMEM((others, 8, 128), jnp.int32),
            [pltpu.VMEM(piece, bf16) for piece in pieces],
            [pltpu.VMEM(piece, bf16) for piece in pieces],
            [pltpu.VMEM((q_count, BLK, span), bf16) for span in spans],
            dma((others,)), dma((others,)),
            dma((head_count - 1,)), dma((head_count - 1,)),
            dma((len(pieces), CHUNKS, others)), dma((len(pieces), CHUNKS, others)),
            dma((len(spans), head_count - 1, per_head)),
            dma((len(spans), head_count - 1, per_head)),
            dma((len(spans), per_head)),
            dma((4,)),
            pltpu.VMEM((q_count, ratio * BLK, HD), jnp.float32),
            pltpu.VMEM((q_count, ratio * BLK, HD), jnp.float32),
            pltpu.VMEM((q_count, ratio * BLK, HD), jnp.float32),
            pltpu.VMEM((q_count, ratio * BLK, far_count * BLK), bf16),
        ],
        compiler_params=pltpu.CompilerParams(
            collective_id=0, has_side_effects=True, vmem_limit_bytes=56 * 2**20
        ),
    )(ids, slots_of, asked, queries, cache_keys.reshape(blocks), cache_values.reshape(blocks))
    return pl.pallas_call(
        functools.partial(side_by_side, head_count, ratio, kv_local - 1),
        grid=(rows // TILE,),
        out_shape=jax.ShapeDtypeStruct((rows, q_columns), bf16),
        in_specs=[pl.BlockSpec((TILE, head_count * span), lambda i: (i, 0)) for span in spans],
        out_specs=pl.BlockSpec((TILE, q_columns), lambda i: (i, 0)),
        compiler_params=pltpu.CompilerParams(vmem_limit_bytes=62 * 2**20),
    )(*landed)


def solution(mesh):
    return jax.shard_map(
        shards,
        mesh=mesh,
        in_specs=(P(("seq", "head"), None), P("seq", "head"), P("seq", "head"), P("seq", None)),
        out_specs=P(("seq", "head"), None),
        check_vma=False,
    )
```
